32 devices in a mesh: groups: 2 (over y), blk: 4 (over z), sub: 2 (over x), pair: 2 (over core).
Axes of the slice: x: 2, y: 2, z: 4, core: 2. Of those that a mesh axis runs over, the one named last changes fastest.
Arguments:
- resid: bfloat16 [512, 8192], P(('groups', 'blk'), ('sub', 'pair')), parts along dimension 0, may hold values from -6 to 6
- context: bfloat16 [512, 8192], P('groups', 'blk'), parts along dimension 0, may hold values from -6 to 6
- w_out: bfloat16 [8192, 8192], P('blk', ('sub', 'pair')), may hold values from -0.0625 to 0.0625
- w_in: bfloat16 [8192, 14336], P(('sub', 'pair'), 'blk'), may hold values from -0.0625 to 0.0625
- w_down: bfloat16 [14336, 8192], P('blk', ('sub', 'pair')), may hold values from -0.046875 to 0.046875
- scales: float32 [3], replicated, may hold values from 0.5 to 2
Outputs:
- result: bfloat16 [512, 8192], P(('groups', 'blk'), ('sub', 'pair')), parts along dimension 0
The draws below stay inside these ranges and needn't reach their ends.
There are 2 independent parts, one for each index of `groups`. The reference program is written for one: setup_inputs(seed, part) draws one part's arguments, and reference() takes and returns one part's arrays. A program takes and returns all parts, laid end to end along the dimension named above; an argument that names none is the same for every part. Nothing has to cross between parts.
All inputs are finite; a program needn't handle non-finite values.
Results may differ from the reference program's by a relative error of at most 0.025.
Values may be sent and summed in bfloat16 or wider, within the bound.
No kernel may reach another device: no remote copies, remote signals or barrier semaphores. Data moves between devices by JAX's collectives and lax.ppermute only.
A program may use at most 128 MiB of HBM per device.

```python
import math
import jax
import jax.numpy as jnp
from jax import lax

D = 8192
HID = 14336
TOKENS = 256
N_BLK = 4
N_SUB = 2
N_PAIR = 2


def steps_of(own_key, extent, shards, smallest, largest):
    factor_of = 1.0
    for dim, blocks in shards:
        heights = jax.random.uniform(jax.random.fold_in(jax.random.fold_in(own_key, 6), dim), (blocks,), jnp.float32, smallest / len(shards), largest / len(shards))
        factor_of = factor_of * jnp.repeat(jnp.exp(heights), extent[dim] // blocks).reshape((-1,) + (1,) * (len(extent) - 1 - dim))
    return factor_of


def scatter_about(stream_key, dims, scale, reach, cuts=(), kind=jnp.bfloat16):
    gain = steps_of(stream_key, dims, cuts, -0.22, 0.18) if cuts else 1.0
    values = jax.random.normal(stream_key, dims, jnp.float32) * scale * gain
    return jnp.minimum(jnp.maximum(values, -reach), reach).astype(kind)


def setup_inputs(seed: int = 0, part: int = 0) -> dict:
    arg_keys = jax.random.split(jax.random.key(seed), 7)
    own_keys = jax.random.split(jax.random.fold_in(arg_keys[6], part), 7)
    return {
        "resid": scatter_about(own_keys[0], (TOKENS, D), 1.0, 6.0, ((0, 4), (1, 4))),
        "context": scatter_about(own_keys[1], (TOKENS, D), 1.0, 6.0, ((1, 4),)),
        "w_out": scatter_about(arg_keys[2], (D, D), D ** -0.5, 0.0625, ((0, 4), (1, 4))),
        "w_in": scatter_about(arg_keys[3], (D, HID), D ** -0.5, 0.0625, ((0, 4), (1, 4))),
        "w_down": scatter_about(arg_keys[4], (HID, D), HID ** -0.5, 0.046875, ((0, 4), (1, 4))),
        "scales": jnp.clip(jnp.exp(jax.random.uniform(arg_keys[5], (3,), jnp.float32, math.log(0.5), math.log(2.0))), 0.5, 2.0),
    }


def block_sum(left, right, parts):
    width = left.shape[1] // parts
    total = jnp.zeros((left.shape[0], right.shape[1]), jnp.float32)
    for index in range(parts):
        term = jnp.dot(left[:, index * width:(index + 1) * width], right[index * width:(index + 1) * width], preferred_element_type=jnp.float32)
        rounded = lax.optimization_barrier(term.astype(jnp.bfloat16))
        total = total + rounded.astype(jnp.float32)
    return total


def reference(resid, context, w_out, w_in, w_down, scales):
    attn = block_sum(context, w_out, N_BLK)
    mixed = (resid.astype(jnp.float32) + scales[0] * attn).astype(jnp.bfloat16)
    pre = block_sum(mixed, w_in, N_SUB * N_PAIR)
    hidden = jax.nn.gelu(scales[1] * pre, approximate=False).astype(jnp.bfloat16)
    mlp = block_sum(hidden, w_down, N_BLK)
    return (mixed.astype(jnp.float32) + scales[2] * mlp).astype(jnp.bfloat16)
```

```python
import jax
import jax.numpy as jnp
from jax import lax
from jax.sharding import PartitionSpec as P

F32 = jnp.float32
BF16 = jnp.bfloat16


def general(resid, context, w_out, w_in, w_down, scales):
    attn = lax.psum_scatter(
        jnp.dot(context, w_out, preferred_element_type=F32).astype(BF16), "blk", scatter_dimension=0, tiled=True
    ).astype(F32)
    mixed = (resid.astype(F32) + scales[0] * attn).astype(BF16)
    pre_terms = jnp.dot(lax.all_gather(mixed, "blk", axis=0, tiled=True), w_in, preferred_element_type=F32)
    pre_part = lax.psum_scatter(
        pre_terms.astype(BF16), ("sub", "pair"), scatter_dimension=0, tiled=True
    ).astype(F32)
    hidden_part = jax.nn.gelu(scales[1] * pre_part, approximate=False).astype(BF16)
    hidden = lax.all_gather(hidden_part, ("sub", "pair"), axis=0, tiled=True)
    mlp = lax.psum_scatter(
        jnp.dot(hidden, w_down, preferred_element_type=F32).astype(BF16), "blk", scatter_dimension=0, tiled=True
    ).astype(F32)
    return (mixed.astype(F32) + scales[2] * mlp).astype(BF16)


def swap(x, axis, size, flip):
    return lax.ppermute(x, axis, [(i, i ^ flip) for i in range(size)])


def halves(x, which):
    width = x.shape[1] // 2
    return (
        lax.dynamic_slice_in_dim(x, which * width, width, 1),
        lax.dynamic_slice_in_dim(x, (1 - which) * width, width, 1),
    )


def joined(own, other, which):
    first = which == 0
    return jnp.concatenate([jnp.where(first, own, other), jnp.where(first, other, own)], axis=1)


def add(a, b):
    return a.astype(F32) + b.astype(F32)


def swapped(resid, context, w_out, w_in, w_down, scales):
    n = 4
    z, core = lax.axis_index("blk"), lax.axis_index("pair")
    odd = z & 1
    rows = resid.shape[0] // 2
    width = w_out.shape[1]
    results = []
    for half in range(2):
        ctx = context.reshape(n, 2, rows, -1)[:, half].reshape(n * rows, -1)
        res = resid[half * rows:(half + 1) * rows].astype(F32)
        attn = scales[0] * jnp.dot(ctx, w_out, preferred_element_type=F32)
        mine = (jnp.arange(n) == z)[:, None, None]
        part = (attn.reshape(n, rows, width) + jnp.where(mine, res[None], 0.0)).reshape(n * rows, width).astype(BF16)
        own, other = halves(part, odd)
        own = add(own, swap(other, "blk", n, 1)).astype(BF16)
        own = add(own, swap(own, "blk", n, 2)).astype(BF16)
        mixed = joined(own, swap(own, "blk", n, 1), odd)
        pre = jnp.dot(mixed, w_in, preferred_element_type=F32).astype(BF16)
        own, other = halves(pre, core)
        own = add(own, swap(other, "pair", 2, 1)).astype(BF16)
        own = add(own, swap(own, "sub", 2, 1))
        own = jax.nn.gelu(scales[1] * own, approximate=False).astype(BF16)
        hidden = joined(own, swap(own, "pair", 2, 1), core)
        mlp = jnp.dot(hidden, w_down, preferred_element_type=F32).astype(BF16).reshape(n, rows, width)

        def of(owner):
            return lax.dynamic_index_in_dim(mlp, owner, 0, keepdims=False)

        total = of(z).astype(F32)
        for flip in (3, 2, 1):
            total = add(total, swap(of(z ^ flip), "blk", n, flip))
        kept = lax.dynamic_slice_in_dim(mixed, z * rows, rows, 0)
        results.append((kept.astype(F32) + scales[2] * total).astype(BF16))
    return jnp.concatenate(results, axis=0)


def solution(mesh):
    shape = dict(mesh.shape)
    fast = shape["blk"] == 4 and shape["sub"] == 2 and shape["pair"] == 2
    in_specs = (
        P(("groups", "blk"), ("sub", "pair")),
        P("groups", "blk"),
        P("blk", ("sub", "pair")),
        P(("sub", "pair"), "blk"),
        P("blk", ("sub", "pair")),
        P(),
    )
    out_specs = P(("groups", "blk"), ("sub", "pair"))
    local = swapped if fast else general
    return jax.shard_map(local, mesh=mesh, in_specs=in_specs, out_specs=out_specs, check_vma=False)
```

```python
import functools

import jax
import jax.numpy as jnp
from jax import lax
from jax.experimental import pallas as pl
from jax.experimental.pallas import tpu as pltpu
from jax.sharding import PartitionSpec as P

F32 = jnp.float32
BF16 = jnp.bfloat16


def general(resid, context, w_out, w_in, w_down, scales):
    attn = lax.psum_scatter(
        jnp.dot(context, w_out, preferred_element_type=F32).astype(BF16), "blk", scatter_dimension=0, tiled=True
    ).astype(F32)
    mixed = (resid.astype(F32) + scales[0] * attn).astype(BF16)
    pre_terms = jnp.dot(lax.all_gather(mixed, "blk", axis=0, tiled=True), w_in, preferred_element_type=F32)
    pre_part = lax.psum_scatter(
        pre_terms.astype(BF16), ("sub", "pair"), scatter_dimension=0, tiled=True
    ).astype(F32)
    hidden_part = jax.nn.gelu(scales[1] * pre_part, approximate=False).astype(BF16)
    hidden = lax.all_gather(hidden_part, ("sub", "pair"), axis=0, tiled=True)
    mlp = lax.psum_scatter(
        jnp.dot(hidden, w_down, preferred_element_type=F32).astype(BF16), "blk", scatter_dimension=0, tiled=True
    ).astype(F32)
    return (mixed.astype(F32) + scales[2] * mlp).astype(BF16)


def swap(x, axis, size, flip):
    return lax.ppermute(x, axis, [(i, i ^ flip) for i in range(size)])


def halves(x, which):
    width = x.shape[1] // 2
    return (
        lax.dynamic_slice_in_dim(x, which * width, width, 1),
        lax.dynamic_slice_in_dim(x, (1 - which) * width, width, 1),
    )


def joined(own, other, which):
    first = which == 0
    return jnp.concatenate([jnp.where(first, own, other), jnp.where(first, other, own)], axis=1)


def add(a, b):
    return a.astype(F32) + b.astype(F32)


def after(x, *done):
    return lax.optimization_barrier((x,) + done)[0]


def in_hbm(x):
    return pltpu.with_memory_space_constraint(x, pltpu.HBM)


ANY = pl.BlockSpec(memory_space=pl.ANY)
SMEM = pl.BlockSpec(memory_space=pltpu.SMEM)
VMEM = pl.BlockSpec(memory_space=pltpu.VMEM)


def out_kernel(n, tile, where, scales, ctx_hbm, w_hbm, res_hbm, first, second, ctx, w, res, sems):
    rows, width = first.shape[1:]
    steps = width // tile
    start = where[1] * width
    loads = [
        pltpu.make_async_copy(ctx_hbm, ctx, sems.at[0]),
        pltpu.make_async_copy(
            res_hbm.at[:, pl.ds(pl.multiple_of(start, width), width)], res, sems.at[1]
        ),
    ]
    for j in range(steps):
        columns = pl.ds(pl.multiple_of(start + j * tile, tile), tile)
        loads.append(pltpu.make_async_copy(w_hbm.at[:, columns], w.at[j], sems.at[2 + j]))
    for load in loads:
        load.start()
    loads[0].wait()
    loads[1].wait()
    for j in range(steps):
        loads[2 + j].wait()
        at = slice(j * tile, (j + 1) * tile)
        term = jnp.dot(ctx[...], w[j], preferred_element_type=F32) * scales[0]
        term = term.reshape(n, 2 * rows, tile)
        mine = lax.broadcasted_iota(jnp.int32, term.shape, 0) == where[0]
        term = (term + jnp.where(mine, res[:, at].astype(F32)[None], 0.0)).astype(BF16)
        first[:, :, at] = term[:, :rows]
        second[:, :, at] = term[:, rows:]


def out_projection(context, w_out, resid, scales, z, which, n):
    depth, width = w_out.shape[0], w_out.shape[1] // 2
    rows = resid.shape[0] // 2
    tile = min(256, width)
    part = jax.ShapeDtypeStruct((n, rows, width), BF16)
    first, second = pl.pallas_call(
        functools.partial(out_kernel, n, tile),
        out_shape=(part, part),
        in_specs=[SMEM, SMEM, ANY, ANY, ANY],
        out_specs=[VMEM, VMEM],
        scratch_shapes=[
            pltpu.VMEM(context.shape, BF16),
            pltpu.VMEM((width // tile, depth, tile), BF16),
            pltpu.VMEM((2 * rows, width), BF16),
            pltpu.SemaphoreType.DMA((2 + width // tile,)),
        ],
        compiler_params=pltpu.CompilerParams(vmem_limit_bytes=16 << 20),
        cost_estimate=pl.CostEstimate(
            flops=2 * context.shape[0] * depth * width, bytes_accessed=2 * depth * width, transcendentals=0
        ),
    )(jnp.stack([z, which]).astype(jnp.int32), scales, in_hbm(context), in_hbm(w_out), in_hbm(resid))
    return first.reshape(n * rows, -1), second.reshape(n * rows, -1)


def fetch_kernel(blocks, which, w_hbm, *rest):
    parts, sems = rest[:-1], rest[-1]
    loads = []
    for index, ((row, column), part) in enumerate(zip(blocks, parts)):
        height, width = part.shape
        at_row = pl.ds(pl.multiple_of(which[row] * height, height), height)
        if column is None:
            source = w_hbm.at[at_row, :]
        else:
            source = w_hbm.at[at_row, pl.ds(pl.multiple_of(which[column] * width, width), width)]
        loads.append(pltpu.make_async_copy(source, part, sems.at[index]))
    for load in loads:
        load.start()
    for load in loads:
        load.wait()


def fetch(w, which, blocks):
    height = w.shape[0] // 2
    parts = [
        pltpu.VMEM((height, w.shape[1] if column is None else w.shape[1] // 2), BF16) for _, column in blocks
    ]
    return pl.pallas_call(
        functools.partial(fetch_kernel, blocks),
        out_shape=parts,
        in_specs=[SMEM, ANY],
        out_specs=[VMEM] * len(blocks),
        scratch_shapes=[pltpu.SemaphoreType.DMA((len(blocks),))],
        compiler_params=pltpu.CompilerParams(vmem_limit_bytes=2 << 20),
        cost_estimate=pl.CostEstimate(flops=0, bytes_accessed=4 * w.size, transcendentals=0),
    )(jnp.stack(which).astype(jnp.int32), in_hbm(w))


def dot(x, w):
    return jnp.dot(x, w, preferred_element_type=F32)


def swapped(resid, context, w_out, w_in, w_down, scales):
    n = 4
    z, core = lax.axis_index("blk"), lax.axis_index("pair")
    odd = z & 1
    rows = resid.shape[0] // 2
    width = w_out.shape[1]
    others = out_projection(context, w_out, resid, scales, z, 1 - odd, n)
    owns = out_projection(context, w_out, resid, scales, z, odd, n)
    results = []
    crossed = moved = down = None
    others = others[0], after(others[1], owns[1])
    summed = [add(owns[half], swap(others[half], "blk", n, 1)).astype(BF16) for half in range(2)]
    near_far, near_near, far_far, far_near = fetch(
        after(w_in, summed[0]), [odd, 1 - odd, core, 1 - core], [(0, 3), (0, 2), (1, 3), (1, 2)]
    )
    down_near, down_far = fetch(after(w_down, near_near), [core, 1 - core], [(0, None), (1, None)])
    results = []
    begun = (near_near, down_near)
    moved = down = None
    for half in range(2):
        crossed = after(swap(summed[half], "blk", n, 2), *begun)
        own = add(summed[half], crossed).astype(BF16)
        first = dot(own, near_far)
        if not half:
            summed[1] = after(summed[1], first)
        far = swap(own, "blk", n, 1)
        mixed = joined(own, far, odd)
        other = (first + dot(far, far_far)).astype(BF16)
        there = swap(other, "pair", 2, 1)
        own = dot(own, near_near) + dot(far, far_near)
        own = add(own, there).astype(BF16)
        if half:
            own = after(own, moved)
        else:
            begun = (own,)
        moved = swap(own, "sub", 2, 1)
        if half:
            moved = after(moved, down)
        own = add(own, moved)
        own = jax.nn.gelu(scales[1] * own, approximate=False).astype(BF16)
        there = swap(own, "pair", 2, 1)
        down = (dot(own, down_near) + dot(there, down_far)).astype(BF16)
        mlp = down.reshape(n, rows, width)

        def of(owner):
            return lax.dynamic_index_in_dim(mlp, owner, 0, keepdims=False)

        total = of(z).astype(F32)
        for flip in (3, 2, 1):
            total = add(total, swap(of(z ^ flip), "blk", n, flip))
        kept = lax.dynamic_slice_in_dim(mixed, z * rows, rows, 0)
        results.append((kept.astype(F32) + scales[2] * total).astype(BF16))
    return jnp.concatenate(results, axis=0)


def solution(mesh):
    shape = dict(mesh.shape)
    fast = shape["blk"] == 4 and shape["sub"] == 2 and shape["pair"] == 2
    in_specs = (
        P(("groups", "blk"), ("sub", "pair")),
        P("groups", "blk"),
        P("blk", ("sub", "pair")),
        P(("sub", "pair"), "blk"),
        P("blk", ("sub", "pair")),
        P(),
    )
    out_specs = P(("groups", "blk"), ("sub", "pair"))
    local = swapped if fast else general
    return jax.shard_map(local, mesh=mesh, in_specs=in_specs, out_specs=out_specs, check_vma=False)
```

```python
import functools
import math

import jax
import jax.numpy as jnp
from jax import lax
from jax.experimental import pallas as pl
from jax.experimental.pallas import tpu as pltpu
from jax.sharding import PartitionSpec as P

F32 = jnp.float32
BF16 = jnp.bfloat16


def general(resid, context, w_out, w_in, w_down, scales):
    attn = lax.psum_scatter(
        jnp.dot(context, w_out, preferred_element_type=F32).astype(BF16), "blk", scatter_dimension=0, tiled=True
    ).astype(F32)
    mixed = (resid.astype(F32) + scales[0] * attn).astype(BF16)
    pre_terms = jnp.dot(lax.all_gather(mixed, "blk", axis=0, tiled=True), w_in, preferred_element_type=F32)
    pre_part = lax.psum_scatter(
        pre_terms.astype(BF16), ("sub", "pair"), scatter_dimension=0, tiled=True
    ).astype(F32)
    hidden_part = jax.nn.gelu(scales[1] * pre_part, approximate=False).astype(BF16)
    hidden = lax.all_gather(hidden_part, ("sub", "pair"), axis=0, tiled=True)
    mlp = lax.psum_scatter(
        jnp.dot(hidden, w_down, preferred_element_type=F32).astype(BF16), "blk", scatter_dimension=0, tiled=True
    ).astype(F32)
    return (mixed.astype(F32) + scales[2] * mlp).astype(BF16)


def swap(x, axis, size, flip):
    return lax.ppermute(x, axis, [(i, i ^ flip) for i in range(size)])


def add(a, b):
    return a.astype(F32) + b.astype(F32)


def dot(x, w):
    return jnp.dot(x, w, preferred_element_type=F32)


def in_hbm(x):
    return pltpu.with_memory_space_constraint(x, pltpu.HBM)


ANY = pl.BlockSpec(memory_space=pl.ANY)
SMEM = pl.BlockSpec(memory_space=pltpu.SMEM)
VMEM = pl.BlockSpec(memory_space=pltpu.VMEM)


def nothing(*refs):
    pass


def after(x, *done):
    return pl.pallas_call(
        nothing,
        out_shape=jax.ShapeDtypeStruct(x.shape, x.dtype),
        in_specs=[ANY] * (1 + len(done)),
        out_specs=ANY,
        input_output_aliases={0: 0},
        compiler_params=pltpu.CompilerParams(vmem_limit_bytes=1 << 20),
    )(x, *done)


def sent(mlp, n):
    z = lax.axis_index("blk")
    blocks = mlp.reshape(n, mlp.shape[0] // n, -1)
    return [swap(lax.dynamic_index_in_dim(blocks, z ^ flip, 0, keepdims=False), "blk", n, flip) for flip in (3, 2, 1)]


def out_kernel(pieces, near, scales_hbm, ctx_hbm, w_hbm, res_hbm, *rest):
    parts, (ctx, w, res, acc, scales, sems) = rest[:-6], rest[-6:]
    depth, width = w.shape
    block = depth // pieces
    tile = min(256, width)
    z = lax.axis_index("blk")
    which = (z & 1) if near else 1 - (z & 1)
    columns = pl.ds(pl.multiple_of(which * width, width), width)
    loads = []
    for k in range(pieces):
        at = pl.ds(k * block, block)
        loads.append(
            (
                pltpu.make_async_copy(ctx_hbm.at[:, at], ctx.at[:, at], sems.at[2 + 2 * k]),
                pltpu.make_async_copy(w_hbm.at[at, columns], w.at[at], sems.at[3 + 2 * k]),
            )
        )
    last = (
        pltpu.make_async_copy(res_hbm.at[:, columns], res, sems.at[0]),
        pltpu.make_async_copy(scales_hbm, scales, sems.at[1]),
    )
    for load in [load for pair in loads for load in pair] + list(last):
        load.start()
    for k in range(pieces):
        for load in loads[k] + (last if k == pieces - 1 else ()):
            load.wait()
        deep = slice(k * block, (k + 1) * block)
        for c in range(width // tile):
            at = slice(c * tile, (c + 1) * tile)
            term = dot(ctx[:, deep], w[deep, at])
            if k:
                term = acc[:, at] + term
            if k < pieces - 1:
                acc[:, at] = term
                continue
            term = (term * scales[0]).reshape(-1, res.shape[0], tile)
            mine = lax.broadcasted_iota(jnp.int32, term.shape, 0) == z
            term = (term + jnp.where(mine, res[:, at].astype(F32)[None], 0.0)).astype(BF16)
            start = 0
            for part in parts:
                part[:, :, at] = term[:, start:start + part.shape[1]]
                start += part.shape[1]


def out_projection(context, w_out, resid, scales, near, sizes):
    depth, width = w_out.shape[0], w_out.shape[1] // 2
    pieces = 8
    n = context.shape[0] // resid.shape[0]
    parts = pl.pallas_call(
        functools.partial(out_kernel, pieces, near),
        out_shape=[jax.ShapeDtypeStruct((n, size, width), BF16) for size in sizes],
        in_specs=[ANY] * 4,
        out_specs=[VMEM] * len(sizes),
        scratch_shapes=[
            pltpu.VMEM(context.shape, BF16),
            pltpu.VMEM((depth, width), BF16),
            pltpu.VMEM((resid.shape[0], width), BF16),
            pltpu.VMEM((context.shape[0], width), F32),
            pltpu.SMEM(scales.shape, F32),
            pltpu.SemaphoreType.DMA((2 + 2 * pieces,)),
        ],
        compiler_params=pltpu.CompilerParams(vmem_limit_bytes=9 << 20),
        cost_estimate=pl.CostEstimate(
            flops=2 * context.shape[0] * depth * width, bytes_accessed=2 * depth * width, transcendentals=0
        ),
    )(in_hbm(scales), in_hbm(context), in_hbm(w_out), in_hbm(resid))
    return [part.reshape(n * size, width) for part, size in zip(parts, sizes)]


def fetch_kernel(w_hbm, done, *rest):
    parts, token, sems = rest[:-2], rest[-2], rest[-1]
    token[...] = jnp.zeros_like(token)
    height, width = parts[0].shape
    odd, core = lax.axis_index("blk") & 1, lax.axis_index("pair")
    blocks = [(odd, 1 - core), (odd, core), (1 - odd, 1 - core), (1 - odd, core)]
    loads = []
    for index, ((row, column), part) in enumerate(zip(blocks, parts)):
        at_row = pl.ds(pl.multiple_of(row * height, height), height)
        at_column = pl.ds(pl.multiple_of(column * width, width), width)
        loads.append(pltpu.make_async_copy(w_hbm.at[at_row, at_column], part, sems.at[index]))
        loads[index].start()
    for load in loads:
        load.wait()


def fetch(w, done):
    part = pltpu.VMEM((w.shape[0] // 2, w.shape[1] // 2), BF16)
    return pl.pallas_call(
        fetch_kernel,
        out_shape=[part] * 4 + [jax.ShapeDtypeStruct((8, 128), F32)],
        in_specs=[ANY, ANY],
        out_specs=[VMEM] * 5,
        scratch_shapes=[pltpu.SemaphoreType.DMA((4,))],
        compiler_params=pltpu.CompilerParams(vmem_limit_bytes=2 << 20),
        cost_estimate=pl.CostEstimate(flops=0, bytes_accessed=1024, transcendentals=0),
    )(in_hbm(w), done)


def gelu_kernel(scales, own, there, out):
    tile = 256
    for start in range(0, out.shape[1], tile):
        at = slice(start, min(start + tile, out.shape[1]))
        v = scales[1] * add(own[:, at], there[:, at])
        out[:, at] = (0.5 * v * (1.0 + lax.erf(v * math.sqrt(0.5)))).astype(BF16)


def gelu(scales, own, there):
    return pl.pallas_call(
        gelu_kernel,
        out_shape=jax.ShapeDtypeStruct(own.shape, BF16),
        in_specs=[SMEM, VMEM, VMEM],
        out_specs=VMEM,
        compiler_params=pltpu.CompilerParams(vmem_limit_bytes=3 << 20),
    )(scales, own, there)


def down_kernel(pieces, hidden, w_hbm, out, w, acc, sems):
    depth, width = w.shape
    block, tile = depth // pieces, min(512, width)
    loads = []
    for k in range(pieces):
        at = pl.ds(k * block, block)
        loads.append(pltpu.make_async_copy(w_hbm.at[at], w.at[at], sems.at[k]))
        loads[k].start()
    for k in range(pieces):
        loads[k].wait()
        deep = slice(k * block, (k + 1) * block)
        for c in range(width // tile):
            at = slice(c * tile, (c + 1) * tile)
            term = dot(hidden[:, deep], w[deep, at])
            if k:
                term = acc[:, at] + term
            if k < pieces - 1:
                acc[:, at] = term
            else:
                out[:, at] = term.astype(BF16)


def down_projection(hidden, w):
    rows, width = hidden.shape[0], w.shape[1]
    pieces = 7
    return pl.pallas_call(
        functools.partial(down_kernel, pieces),
        out_shape=jax.ShapeDtypeStruct((rows, width), BF16),
        in_specs=[VMEM, ANY],
        out_specs=VMEM,
        scratch_shapes=[
            pltpu.VMEM(w.shape, BF16),
            pltpu.VMEM((rows, width), F32),
            pltpu.SemaphoreType.DMA((pieces,)),
        ],
        compiler_params=pltpu.CompilerParams(vmem_limit_bytes=18 << 20),
        cost_estimate=pl.CostEstimate(flops=2 * rows * w.size, bytes_accessed=2 * w.size, transcendentals=0),
    )(hidden, in_hbm(w))


def end_kernel(scales, done, near, far, mlp, first, second, third, out):
    z = lax.axis_index("blk")
    odd = (z & 1) == 1
    size, width = first.shape[0], out.shape[1] // 2
    rows = pl.ds(pl.multiple_of(z * size, size), size)
    head = out.shape[0] - size
    out[:head, :] = done[...]
    for part in range(2):
        at = slice(part * width, (part + 1) * width)
        total = mlp[rows, at].astype(F32)
        for term in (first, second, third):
            total = total + term[:, at].astype(F32)
        other, own = (far, near) if part == 0 else (near, far)
        mixed = jnp.where(odd, other[rows, :].astype(F32), own[rows, :].astype(F32))
        out[head:, at] = (mixed + scales[2] * total).astype(BF16)


def end(scales, done, near, far, mlp, terms):
    rows, width = done.shape[0] + terms[0].shape[0], done.shape[1]
    return pl.pallas_call(
        end_kernel,
        out_shape=jax.ShapeDtypeStruct((rows, width), BF16),
        in_specs=[SMEM] + [VMEM] * 7,
        out_specs=VMEM,
        compiler_params=pltpu.CompilerParams(vmem_limit_bytes=3 << 20),
    )(scales, done, near, far, mlp, *terms)


def swapped(resid, context, w_out, w_in, w_down, scales):
    n = 4
    z, core = lax.axis_index("blk"), lax.axis_index("pair")
    odd = (z & 1) == 1
    rows = resid.shape[0] // 2
    sizes = [rows, rows]

    other_a, other_b = out_projection(context, w_out, resid, scales, False, sizes)
    own_a, own_b = out_projection(context, w_out, resid, scales, True, sizes)
    other_b = after(other_b, own_a)
    sum_a = add(own_a, swap(other_a, "blk", n, 1)).astype(BF16)
    sum_b = add(own_b, swap(other_b, "blk", n, 1)).astype(BF16)
    near_far, near_near, far_far, far_near, fetched = fetch(w_in, sum_a)

    crossed = after(swap(sum_a, "blk", n, 2), fetched, sum_b)
    near_a = add(sum_a, crossed).astype(BF16)
    first = dot(near_a, near_far)
    sum_b = after(sum_b, first)
    far_a = swap(near_a, "blk", n, 1)
    crossed = swap(sum_b, "blk", n, 2)
    other = (first + dot(far_a, far_far)).astype(BF16)
    mine = dot(near_a, near_near) + dot(far_a, far_near)
    mine_a = add(mine, swap(other, "pair", 2, 1)).astype(BF16)

    crossed = after(crossed, other)
    near_b = add(sum_b, crossed).astype(BF16)
    width = mine_a.shape[1] // 2
    left_a = swap(mine_a[:, :width], "sub", 2, 1)
    right_a = swap(mine_a[:, width:], "sub", 2, 1)
    far_b = after(swap(near_b, "blk", n, 1), left_a)
    mine = dot(near_b, near_near)
    first = dot(near_b, near_far)
    far_b = after(far_b, mine, first)
    mine = mine + dot(far_b, far_near)
    other = (first + dot(far_b, far_far)).astype(BF16)
    there = lax.dynamic_index_in_dim(lax.all_gather(other, "pair", axis=0), 1 - core, 0, keepdims=False)
    mine_b = add(mine, there).astype(BF16)
    right_a = after(right_a, mine_b)
    mine_b = after(mine_b, right_a)
    moved_b = swap(mine_b, "sub", 2, 1)

    hidden = gelu(scales, mine_a, jnp.concatenate([left_a, right_a], axis=1))
    there = swap(hidden, "pair", 2, 1)
    first_core = core == 0
    hidden = jnp.concatenate([jnp.where(first_core, hidden, there), jnp.where(first_core, there, hidden)], axis=1)
    mlp_a = down_projection(hidden, w_down)
    terms_a = sent(mlp_a, n)
    kept = [lax.dynamic_slice_in_dim(part, z * rows, rows, 0) for part in (near_a, far_a)]
    kept = jnp.concatenate([jnp.where(odd, kept[1], kept[0]), jnp.where(odd, kept[0], kept[1])], axis=1)
    total = lax.dynamic_slice_in_dim(mlp_a, z * rows, rows, 0).astype(F32)
    for term in terms_a:
        total = total + term.astype(F32)
    done = (kept.astype(F32) + scales[2] * total).astype(BF16)

    hidden = gelu(scales, mine_b, after(moved_b, mlp_a))
    hidden = lax.all_gather(hidden, "pair", axis=0)
    mlp_b = dot(jnp.concatenate([hidden[0], hidden[1]], axis=1), w_down).astype(BF16)
    return end(scales, done, near_b, far_b, mlp_b, sent(mlp_b, n))


def solution(mesh):
    shape = dict(mesh.shape)
    fast = shape["blk"] == 4 and shape["sub"] == 2 and shape["pair"] == 2
    in_specs = (
        P(("groups", "blk"), ("sub", "pair")),
        P("groups", "blk"),
        P("blk", ("sub", "pair")),
        P(("sub", "pair"), "blk"),
        P("blk", ("sub", "pair")),
        P(),
    )
    out_specs = P(("groups", "blk"), ("sub", "pair"))
    local = swapped if fast else general
    return jax.shard_map(local, mesh=mesh, in_specs=in_specs, out_specs=out_specs, check_vma=False)
```

```python
import functools
import math

import jax
import jax.numpy as jnp
from jax import lax
from jax.experimental import pallas as pl
from jax.experimental.pallas import tpu as pltpu
from jax.sharding import PartitionSpec as P

F32 = jnp.float32
BF16 = jnp.bfloat16


def general(resid, context, w_out, w_in, w_down, scales):
    attn = lax.psum_scatter(
        jnp.dot(context, w_out, preferred_element_type=F32).astype(BF16), "blk", scatter_dimension=0, tiled=True
    ).astype(F32)
    mixed = (resid.astype(F32) + scales[0] * attn).astype(BF16)
    pre_terms = jnp.dot(lax.all_gather(mixed, "blk", axis=0, tiled=True), w_in, preferred_element_type=F32)
    pre_part = lax.psum_scatter(
        pre_terms.astype(BF16), ("sub", "pair"), scatter_dimension=0, tiled=True
    ).astype(F32)
    hidden_part = jax.nn.gelu(scales[1] * pre_part, approximate=False).astype(BF16)
    hidden = lax.all_gather(hidden_part, ("sub", "pair"), axis=0, tiled=True)
    mlp = lax.psum_scatter(
        jnp.dot(hidden, w_down, preferred_element_type=F32).astype(BF16), "blk", scatter_dimension=0, tiled=True
    ).astype(F32)
    return (mixed.astype(F32) + scales[2] * mlp).astype(BF16)


def swap(x, axis, size, flip):
    return lax.ppermute(x, axis, [(i, i ^ flip) for i in range(size)])


def add(a, b):
    return a.astype(F32) + b.astype(F32)


def dot(x, w):
    return jnp.dot(x, w, preferred_element_type=F32)


def in_hbm(x):
    return pltpu.with_memory_space_constraint(x, pltpu.HBM)


ANY = pl.BlockSpec(memory_space=pl.ANY)
SMEM = pl.BlockSpec(memory_space=pltpu.SMEM)
VMEM = pl.BlockSpec(memory_space=pltpu.VMEM)


def nothing(*refs):
    pass


def after(x, *done):
    return pl.pallas_call(
        nothing,
        out_shape=jax.ShapeDtypeStruct(x.shape, x.dtype),
        in_specs=[ANY] * (1 + len(done)),
        out_specs=ANY,
        input_output_aliases={0: 0},
        compiler_params=pltpu.CompilerParams(vmem_limit_bytes=1 << 20),
    )(x, *done)


def sent(mlp, n):
    z = lax.axis_index("blk")
    blocks = mlp.reshape(n, mlp.shape[0] // n, -1)
    return [swap(lax.dynamic_index_in_dim(blocks, z ^ flip, 0, keepdims=False), "blk", n, flip) for flip in (3, 2, 1)]


def sent_by_two(mlp, n):
    z = lax.axis_index("blk")
    blocks = mlp.reshape(n, mlp.shape[0] // n, -1)

    def of(flip):
        return lax.dynamic_index_in_dim(blocks, z ^ flip, 0, keepdims=False)

    joint = swap(of(3), "blk", n, 1)
    term = swap(of(1), "blk", n, 1)
    return [term, swap(add(of(2), joint).astype(BF16), "blk", n, 2)]


def out_kernel(pieces, near, scales_hbm, ctx_hbm, w_hbm, res_hbm, *rest):
    parts, gains, (ctx, w, res, acc, scales, sems) = rest[:-8], rest[-8:-6], rest[-6:]
    depth, width = w.shape
    block = depth // pieces
    tile = min(256, width)
    z = lax.axis_index("blk")
    which = (z & 1) if near else 1 - (z & 1)
    columns = pl.ds(pl.multiple_of(which * width, width), width)
    loads = []
    for k in range(pieces):
        at = pl.ds(k * block, block)
        loads.append(
            (
                pltpu.make_async_copy(ctx_hbm.at[:, at], ctx.at[:, at], sems.at[2 + 2 * k]),
                pltpu.make_async_copy(w_hbm.at[at, columns], w.at[at], sems.at[3 + 2 * k]),
            )
        )
    last = (
        pltpu.make_async_copy(res_hbm.at[:, columns], res, sems.at[0]),
        pltpu.make_async_copy(scales_hbm, scales, sems.at[1]),
    )
    for load in [load for pair in loads for load in pair] + list(last):
        load.start()
    for k in range(pieces):
        for load in loads[k] + (last if k == pieces - 1 else ()):
            load.wait()
        deep = slice(k * block, (k + 1) * block)
        for c in range(width // tile):
            at = slice(c * tile, (c + 1) * tile)
            term = dot(ctx[:, deep], w[deep, at])
            if k:
                term = acc[:, at] + term
            if k < pieces - 1:
                acc[:, at] = term
                continue
            term = (term * scales[0]).reshape(-1, res.shape[0], tile)
            mine = lax.broadcasted_iota(jnp.int32, term.shape, 0) == z
            term = (term + jnp.where(mine, res[:, at].astype(F32)[None], 0.0)).astype(BF16)
            start = 0
            for part in parts:
                part[:, :, at] = term[:, start:start + part.shape[1]]
                start += part.shape[1]
    for index, gain in enumerate(gains):
        gain[...] = jnp.full_like(gain, scales[1 + index])


def out_projection(context, w_out, resid, scales, near, sizes):
    depth, width = w_out.shape[0], w_out.shape[1] // 2
    pieces = 8
    n = context.shape[0] // resid.shape[0]
    gain = jax.ShapeDtypeStruct((8, 128), F32)
    *parts, gain_in, gain_down = pl.pallas_call(
        functools.partial(out_kernel, pieces, near),
        out_shape=[jax.ShapeDtypeStruct((n, size, width), BF16) for size in sizes] + [gain, gain],
        in_specs=[ANY] * 4,
        out_specs=[VMEM] * (len(sizes) + 2),
        scratch_shapes=[
            pltpu.VMEM(context.shape, BF16),
            pltpu.VMEM((depth, width), BF16),
            pltpu.VMEM((resid.shape[0], width), BF16),
            pltpu.VMEM((context.shape[0], width), F32),
            pltpu.SMEM(scales.shape, F32),
            pltpu.SemaphoreType.DMA((2 + 2 * pieces,)),
        ],
        compiler_params=pltpu.CompilerParams(vmem_limit_bytes=9 << 20),
        cost_estimate=pl.CostEstimate(
            flops=2 * context.shape[0] * depth * width, bytes_accessed=2 * depth * width, transcendentals=0
        ),
    )(in_hbm(scales), in_hbm(context), in_hbm(w_out), in_hbm(resid))
    return [part.reshape(n * size, width) for part, size in zip(parts, sizes)] + [gain_in, gain_down]


def fetch_kernel(w_hbm, done, *rest):
    parts, token, sems = rest[:-2], rest[-2], rest[-1]
    token[...] = jnp.zeros_like(token)
    height, width = parts[0].shape
    odd, core = lax.axis_index("blk") & 1, lax.axis_index("pair")
    blocks = [(odd, 1 - core), (odd, core), (1 - odd, 1 - core), (1 - odd, core)]
    loads = []
    for index, ((row, column), part) in enumerate(zip(blocks, parts)):
        at_row = pl.ds(pl.multiple_of(row * height, height), height)
        at_column = pl.ds(pl.multiple_of(column * width, width), width)
        loads.append(pltpu.make_async_copy(w_hbm.at[at_row, at_column], part, sems.at[index]))
        loads[index].start()
    for load in loads:
        load.wait()


def fetch(w, done):
    part = pltpu.VMEM((w.shape[0] // 2, w.shape[1] // 2), BF16)
    return pl.pallas_call(
        fetch_kernel,
        out_shape=[part] * 4 + [jax.ShapeDtypeStruct((8, 128), F32)],
        in_specs=[ANY, ANY],
        out_specs=[VMEM] * 5,
        scratch_shapes=[pltpu.SemaphoreType.DMA((4,))],
        compiler_params=pltpu.CompilerParams(vmem_limit_bytes=2 << 20),
        cost_estimate=pl.CostEstimate(flops=0, bytes_accessed=1024, transcendentals=0),
    )(in_hbm(w), done)


def gelu_kernel(gain, own, there, out):
    tile = 256
    for start in range(0, out.shape[1], tile):
        at = slice(start, min(start + tile, out.shape[1]))
        v = gain[:1, :1] * add(own[:, at], there[:, at])
        out[:, at] = (0.5 * v * (1.0 + lax.erf(v * math.sqrt(0.5)))).astype(BF16)


def gelu(gain, own, there):
    return pl.pallas_call(
        gelu_kernel,
        out_shape=jax.ShapeDtypeStruct(own.shape, BF16),
        in_specs=[VMEM] * 3,
        out_specs=VMEM,
        compiler_params=pltpu.CompilerParams(vmem_limit_bytes=3 << 20),
    )(gain, own, there)


def down_kernel(pieces, hidden, w_hbm, out, w, acc, sems):
    depth, width = w.shape
    block, tile = depth // pieces, min(512, width)
    loads = []
    for k in range(pieces):
        at = pl.ds(k * block, block)
        loads.append(pltpu.make_async_copy(w_hbm.at[at], w.at[at], sems.at[k]))
        loads[k].start()
    for k in range(pieces):
        loads[k].wait()
        deep = slice(k * block, (k + 1) * block)
        for c in range(width // tile):
            at = slice(c * tile, (c + 1) * tile)
            term = dot(hidden[:, deep], w[deep, at])
            if k:
                term = acc[:, at] + term
            if k < pieces - 1:
                acc[:, at] = term
            else:
                out[:, at] = term.astype(BF16)


def down_projection(hidden, w):
    rows, width = hidden.shape[0], w.shape[1]
    pieces = 7
    return pl.pallas_call(
        functools.partial(down_kernel, pieces),
        out_shape=jax.ShapeDtypeStruct((rows, width), BF16),
        in_specs=[VMEM, ANY],
        out_specs=VMEM,
        scratch_shapes=[
            pltpu.VMEM(w.shape, BF16),
            pltpu.VMEM((rows, width), F32),
            pltpu.SemaphoreType.DMA((pieces,)),
        ],
        compiler_params=pltpu.CompilerParams(vmem_limit_bytes=18 << 20),
        cost_estimate=pl.CostEstimate(flops=2 * rows * w.size, bytes_accessed=2 * w.size, transcendentals=0),
    )(hidden, in_hbm(w))


def end_kernel(gain, done, near, far, mlp, first, second, third, out):
    z = lax.axis_index("blk")
    odd = (z & 1) == 1
    size, width = first.shape[0], out.shape[1] // 2
    rows = pl.ds(pl.multiple_of(z * size, size), size)
    head = out.shape[0] - size
    out[:head, :] = done[...]
    for part in range(2):
        at = slice(part * width, (part + 1) * width)
        total = mlp[rows, at].astype(F32)
        for term in (first, second, third):
            total = total + term[:, at].astype(F32)
        other, own = (far, near) if part == 0 else (near, far)
        mixed = jnp.where(odd, other[rows, :].astype(F32), own[rows, :].astype(F32))
        out[head:, at] = (mixed + gain[:1, :1] * total).astype(BF16)


def end(gain, done, near, far, mlp, terms):
    rows, width = done.shape[0] + terms[0].shape[0], done.shape[1]
    return pl.pallas_call(
        end_kernel,
        out_shape=jax.ShapeDtypeStruct((rows, width), BF16),
        in_specs=[VMEM] * 8,
        out_specs=VMEM,
        compiler_params=pltpu.CompilerParams(vmem_limit_bytes=3 << 20),
    )(gain, done, near, far, mlp, *terms)


def swapped(resid, context, w_out, w_in, w_down, scales):
    n = 4
    z, core = lax.axis_index("blk"), lax.axis_index("pair")
    odd = (z & 1) == 1
    rows = resid.shape[0] // 2
    sizes = [rows, rows]

    other_a, other_b, _, _ = out_projection(context, w_out, resid, scales, False, sizes)
    own_a, own_b, gain_in, gain_down = out_projection(context, w_out, resid, scales, True, sizes)
    other_b = after(other_b, own_a)
    sum_a = add(own_a, swap(other_a, "blk", n, 1)).astype(BF16)
    sum_b = add(own_b, swap(other_b, "blk", n, 1)).astype(BF16)
    near_far, near_near, far_far, far_near, fetched = fetch(w_in, sum_a)

    crossed = after(swap(sum_a, "blk", n, 2), fetched, sum_b)
    near_a = add(sum_a, crossed).astype(BF16)
    first = dot(near_a, near_far)
    sum_b = after(sum_b, first)
    far_a = swap(near_a, "blk", n, 1)
    crossed = swap(sum_b, "blk", n, 2)
    other = (first + dot(far_a, far_far)).astype(BF16)
    mine = dot(near_a, near_near)
    early = mine
    mine = mine + dot(far_a, far_near)
    mine_a = add(mine, swap(other, "pair", 2, 1)).astype(BF16)

    crossed = after(crossed, other, early)
    near_b = add(sum_b, crossed).astype(BF16)
    width = mine_a.shape[1] // 2
    left_a = swap(mine_a[:, :width], "sub", 2, 1)
    right_a = swap(mine_a[:, width:], "sub", 2, 1)
    far_b = after(swap(near_b, "blk", n, 1), left_a)
    mine = dot(near_b, near_near)
    first = dot(near_b, near_far)
    far_b = after(far_b, mine, first)
    mine = mine + dot(far_b, far_near)
    other = (first + dot(far_b, far_far)).astype(BF16)
    there = lax.dynamic_index_in_dim(lax.all_gather(other, "pair", axis=0), 1 - core, 0, keepdims=False)
    mine_b = add(mine, there).astype(BF16)
    right_a = after(right_a, mine_b)
    mine_b = after(mine_b, right_a)
    moved_b = swap(mine_b, "sub", 2, 1)

    hidden = gelu(gain_in, mine_a, jnp.concatenate([left_a, right_a], axis=1))
    there = swap(hidden, "pair", 2, 1)
    first_core = core == 0
    hidden = jnp.concatenate([jnp.where(first_core, hidden, there), jnp.where(first_core, there, hidden)], axis=1)
    mlp_a = down_projection(hidden, w_down)
    terms_a = sent(mlp_a, n)
    kept = [lax.dynamic_slice_in_dim(part, z * rows, rows, 0) for part in (near_a, far_a)]
    kept = jnp.concatenate([jnp.where(odd, kept[1], kept[0]), jnp.where(odd, kept[0], kept[1])], axis=1)
    total = lax.dynamic_slice_in_dim(mlp_a, z * rows, rows, 0).astype(F32)
    for term in terms_a:
        total = total + term.astype(F32)
    done = (kept.astype(F32) + gain_down[:1, :1] * total).astype(BF16)

    hidden = gelu(gain_in, mine_b, after(moved_b, mlp_a))
    hidden = lax.all_gather(hidden, "pair", axis=0)
    mlp_b = dot(jnp.concatenate([hidden[0], hidden[1]], axis=1), w_down).astype(BF16)
    return end(gain_down, done, near_b, far_b, mlp_b, sent(mlp_b, n))


def solution(mesh):
    shape = dict(mesh.shape)
    fast = shape["blk"] == 4 and shape["sub"] == 2 and shape["pair"] == 2
    in_specs = (
        P(("groups", "blk"), ("sub", "pair")),
        P("groups", "blk"),
        P("blk", ("sub", "pair")),
        P(("sub", "pair"), "blk"),
        P("blk", ("sub", "pair")),
        P(),
    )
    out_specs = P(("groups", "blk"), ("sub", "pair"))
    local = swapped if fast else general
    return jax.shard_map(local, mesh=mesh, in_specs=in_specs, out_specs=out_specs, check_vma=False)
```

```python
import functools
import math

import jax
import jax.numpy as jnp
from jax import lax
from jax.experimental import pallas as pl
from jax.experimental.pallas import tpu as pltpu
from jax.sharding import PartitionSpec as P

F32 = jnp.float32
BF16 = jnp.bfloat16


def general(resid, context, w_out, w_in, w_down, scales):
    attn = lax.psum_scatter(
        jnp.dot(context, w_out, preferred_element_type=F32).astype(BF16), "blk", scatter_dimension=0, tiled=True
    ).astype(F32)
    mixed = (resid.astype(F32) + scales[0] * attn).astype(BF16)
    pre_terms = jnp.dot(lax.all_gather(mixed, "blk", axis=0, tiled=True), w_in, preferred_element_type=F32)
    pre_part = lax.psum_scatter(
        pre_terms.astype(BF16), ("sub", "pair"), scatter_dimension=0, tiled=True
    ).astype(F32)
    hidden_part = jax.nn.gelu(scales[1] * pre_part, approximate=False).astype(BF16)
    hidden = lax.all_gather(hidden_part, ("sub", "pair"), axis=0, tiled=True)
    mlp = lax.psum_scatter(
        jnp.dot(hidden, w_down, preferred_element_type=F32).astype(BF16), "blk", scatter_dimension=0, tiled=True
    ).astype(F32)
    return (mixed.astype(F32) + scales[2] * mlp).astype(BF16)


def swap(x, axis, size, flip):
    return lax.ppermute(x, axis, [(i, i ^ flip) for i in range(size)])


def add(a, b):
    return a.astype(F32) + b.astype(F32)


def dot(x, w):
    return jnp.dot(x, w, preferred_element_type=F32)


def in_hbm(x):
    return pltpu.with_memory_space_constraint(x, pltpu.HBM)


ANY = pl.BlockSpec(memory_space=pl.ANY)
SMEM = pl.BlockSpec(memory_space=pltpu.SMEM)
VMEM = pl.BlockSpec(memory_space=pltpu.VMEM)


def nothing(*refs):
    pass


def after(x, *done):
    return pl.pallas_call(
        nothing,
        out_shape=jax.ShapeDtypeStruct(x.shape, x.dtype),
        in_specs=[ANY] * (1 + len(done)),
        out_specs=ANY,
        input_output_aliases={0: 0},
        compiler_params=pltpu.CompilerParams(vmem_limit_bytes=1 << 20),
    )(x, *done)


def sent(mlp, n):
    z = lax.axis_index("blk")
    blocks = mlp.reshape(n, mlp.shape[0] // n, -1)
    return [swap(lax.dynamic_index_in_dim(blocks, z ^ flip, 0, keepdims=False), "blk", n, flip) for flip in (3, 2, 1)]


def sent_by_two(mlp, n):
    z = lax.axis_index("blk")
    blocks = mlp.reshape(n, mlp.shape[0] // n, -1)

    def of(flip):
        return lax.dynamic_index_in_dim(blocks, z ^ flip, 0, keepdims=False)

    joint = swap(of(3), "blk", n, 1)
    term = swap(of(1), "blk", n, 1)
    return [term, swap(add(of(2), joint).astype(BF16), "blk", n, 2)]


def out_kernel(pieces, near, scales_hbm, ctx_hbm, w_hbm, res_hbm, *rest):
    parts, gains, (ctx, w, res, acc, scales, sems) = rest[:-8], rest[-8:-6], rest[-6:]
    depth, width = w.shape
    block = depth // pieces
    tile = min(256, width)
    z = lax.axis_index("blk")
    which = (z & 1) if near else 1 - (z & 1)
    columns = pl.ds(pl.multiple_of(which * width, width), width)
    loads = []
    for k in range(pieces):
        at = pl.ds(k * block, block)
        loads.append(
            (
                pltpu.make_async_copy(ctx_hbm.at[:, at], ctx.at[:, at], sems.at[2 + 2 * k]),
                pltpu.make_async_copy(w_hbm.at[at, columns], w.at[at], sems.at[3 + 2 * k]),
            )
        )
    last = (
        pltpu.make_async_copy(res_hbm.at[:, columns], res, sems.at[0]),
        pltpu.make_async_copy(scales_hbm, scales, sems.at[1]),
    )
    for load in [load for pair in loads for load in pair] + list(last):
        load.start()
    for k in range(pieces):
        for load in loads[k] + (last if k == pieces - 1 else ()):
            load.wait()
        deep = slice(k * block, (k + 1) * block)
        for c in range(width // tile):
            at = slice(c * tile, (c + 1) * tile)
            term = dot(ctx[:, deep], w[deep, at])
            if k:
                term = acc[:, at] + term
            if k < pieces - 1:
                acc[:, at] = term
                continue
            term = (term * scales[0]).reshape(-1, res.shape[0], tile)
            mine = lax.broadcasted_iota(jnp.int32, term.shape, 0) == z
            term = (term + jnp.where(mine, res[:, at].astype(F32)[None], 0.0)).astype(BF16)
            start = 0
            for part in parts:
                part[:, :, at] = term[:, start:start + part.shape[1]]
                start += part.shape[1]
    for index, gain in enumerate(gains):
        gain[...] = jnp.full_like(gain, scales[1 + index])


def out_projection(context, w_out, resid, scales, near, sizes):
    depth, width = w_out.shape[0], w_out.shape[1] // 2
    pieces = depth // 256
    n = context.shape[0] // resid.shape[0]
    gains = [jax.ShapeDtypeStruct((1, 128), F32), jax.ShapeDtypeStruct((1, 2 * width), F32)]
    *parts, gain_in, gain_down = pl.pallas_call(
        functools.partial(out_kernel, pieces, near),
        out_shape=[jax.ShapeDtypeStruct((n, size, width), BF16) for size in sizes] + gains,
        in_specs=[ANY] * 4,
        out_specs=[VMEM] * (len(sizes) + 2),
        scratch_shapes=[
            pltpu.VMEM(context.shape, BF16),
            pltpu.VMEM((depth, width), BF16),
            pltpu.VMEM((resid.shape[0], width), BF16),
            pltpu.VMEM((context.shape[0], width), F32),
            pltpu.SMEM(scales.shape, F32),
            pltpu.SemaphoreType.DMA((2 + 2 * pieces,)),
        ],
        compiler_params=pltpu.CompilerParams(vmem_limit_bytes=9 << 20),
        cost_estimate=pl.CostEstimate(
            flops=2 * context.shape[0] * depth * width, bytes_accessed=2 * depth * width, transcendentals=0
        ),
    )(in_hbm(scales), in_hbm(context), in_hbm(w_out), in_hbm(resid))
    return [part.reshape(n * size, width) for part, size in zip(parts, sizes)] + [gain_in, gain_down]


def fetch_kernel(w_hbm, done, *rest):
    parts, token, sems = rest[:-2], rest[-2], rest[-1]
    token[...] = jnp.zeros_like(token)
    height, width = parts[0].shape
    odd, core = lax.axis_index("blk") & 1, lax.axis_index("pair")
    blocks = [(odd, 1 - core), (odd, core), (1 - odd, 1 - core), (1 - odd, core)]
    loads = []
    for index, ((row, column), part) in enumerate(zip(blocks, parts)):
        at_row = pl.ds(pl.multiple_of(row * height, height), height)
        at_column = pl.ds(pl.multiple_of(column * width, width), width)
        loads.append(pltpu.make_async_copy(w_hbm.at[at_row, at_column], part, sems.at[index]))
        loads[index].start()
    for load in loads:
        load.wait()


def fetch(w, done):
    part = pltpu.VMEM((w.shape[0] // 2, w.shape[1] // 2), BF16)
    return pl.pallas_call(
        fetch_kernel,
        out_shape=[part] * 4 + [jax.ShapeDtypeStruct((8, 128), F32)],
        in_specs=[ANY, ANY],
        out_specs=[VMEM] * 5,
        scratch_shapes=[pltpu.SemaphoreType.DMA((4,))],
        compiler_params=pltpu.CompilerParams(vmem_limit_bytes=2 << 20),
        cost_estimate=pl.CostEstimate(flops=0, bytes_accessed=1024, transcendentals=0),
    )(in_hbm(w), done)


def gelu_kernel(gain, own, there, out):
    tile = 256
    for start in range(0, out.shape[1], tile):
        at = slice(start, min(start + tile, out.shape[1]))
        v = gain[:1, :1] * add(own[:, at], there[:, at])
        out[:, at] = (0.5 * v * (1.0 + lax.erf(v * math.sqrt(0.5)))).astype(BF16)


def gelu(gain, own, there):
    return pl.pallas_call(
        gelu_kernel,
        out_shape=jax.ShapeDtypeStruct(own.shape, BF16),
        in_specs=[VMEM] * 3,
        out_specs=VMEM,
        compiler_params=pltpu.CompilerParams(vmem_limit_bytes=3 << 20),
    )(gain, own, there)


def down_kernel(pieces, hidden, w_hbm, out, w, acc, sems):
    depth, width = w.shape
    block, tile = depth // pieces, min(512, width)
    loads = []
    for k in range(pieces):
        at = pl.ds(k * block, block)
        loads.append(pltpu.make_async_copy(w_hbm.at[at], w.at[at], sems.at[k]))
        loads[k].start()
    for k in range(pieces):
        loads[k].wait()
        deep = slice(k * block, (k + 1) * block)
        for c in range(width // tile):
            at = slice(c * tile, (c + 1) * tile)
            term = dot(hidden[:, deep], w[deep, at])
            if k:
                term = acc[:, at] + term
            if k < pieces - 1:
                acc[:, at] = term
            else:
                out[:, at] = term.astype(BF16)


def down_projection(hidden, w):
    rows, width = hidden.shape[0], w.shape[1]
    pieces = w.shape[0] // 256
    return pl.pallas_call(
        functools.partial(down_kernel, pieces),
        out_shape=jax.ShapeDtypeStruct((rows, width), BF16),
        in_specs=[VMEM, ANY],
        out_specs=VMEM,
        scratch_shapes=[
            pltpu.VMEM(w.shape, BF16),
            pltpu.VMEM((rows, width), F32),
            pltpu.SemaphoreType.DMA((pieces,)),
        ],
        compiler_params=pltpu.CompilerParams(vmem_limit_bytes=18 << 20),
        cost_estimate=pl.CostEstimate(flops=2 * rows * w.size, bytes_accessed=2 * w.size, transcendentals=0),
    )(hidden, in_hbm(w))


def end_kernel(gain, done, near, far, mlp, first, second, third, out):
    z = lax.axis_index("blk")
    odd = (z & 1) == 1
    size, width = first.shape[0], out.shape[1] // 2
    rows = pl.ds(pl.multiple_of(z * size, size), size)
    head = out.shape[0] - size
    out[:head, :] = done[...]
    for part in range(2):
        at = slice(part * width, (part + 1) * width)
        total = mlp[rows, at].astype(F32)
        for term in (first, second, third):
            total = total + term[:, at].astype(F32)
        other, own = (far, near) if part == 0 else (near, far)
        mixed = jnp.where(odd, other[rows, :].astype(F32), own[rows, :].astype(F32))
        out[head:, at] = (mixed + gain[:1, :1] * total).astype(BF16)


def end(gain, done, near, far, mlp, terms):
    rows, width = done.shape[0] + terms[0].shape[0], done.shape[1]
    return pl.pallas_call(
        end_kernel,
        out_shape=jax.ShapeDtypeStruct((rows, width), BF16),
        in_specs=[VMEM] * 8,
        out_specs=VMEM,
        compiler_params=pltpu.CompilerParams(vmem_limit_bytes=3 << 20),
    )(gain, done, near, far, mlp, *terms)


def swapped(resid, context, w_out, w_in, w_down, scales):
    n = 4
    z, core = lax.axis_index("blk"), lax.axis_index("pair")
    odd = (z & 1) == 1
    rows = resid.shape[0] // 2
    sizes = [rows, rows]

    other_a, other_b, _, _ = out_projection(context, w_out, resid, scales, False, sizes)
    own_a, own_b, gain_in, gain_down = out_projection(context, w_out, resid, scales, True, sizes)
    other_b = after(other_b, own_a)
    sum_a = add(own_a, swap(other_a, "blk", n, 1)).astype(BF16)
    sum_b = add(own_b, swap(other_b, "blk", n, 1)).astype(BF16)
    near_far, near_near, far_far, far_near, fetched = fetch(w_in, sum_a)

    crossed = after(swap(sum_a, "blk", n, 2), fetched, sum_b)
    near_a = add(sum_a, crossed).astype(BF16)
    first = dot(near_a, near_far)
    sum_b = after(sum_b, first)
    far_a = swap(near_a, "blk", n, 1)
    crossed = swap(sum_b, "blk", n, 2)
    other = (first + dot(far_a, far_far)).astype(BF16)
    mine = dot(near_a, near_near)
    early = mine
    mine = mine + dot(far_a, far_near)
    mine_a = add(mine, swap(other, "pair", 2, 1)).astype(BF16)

    crossed = after(crossed, other, early)
    near_b = add(sum_b, crossed).astype(BF16)
    width = mine_a.shape[1] // 128 * 3 // 8 * 128
    left_a = swap(mine_a[:, :width], "sub", 2, 1)
    right_a = swap(mine_a[:, width:], "sub", 2, 1)
    far_b = after(swap(near_b, "blk", n, 1), left_a)
    mine = dot(near_b, near_near)
    first = dot(near_b, near_far)
    far_b = after(far_b, mine, first)
    mine = mine + dot(far_b, far_near)
    other = (first + dot(far_b, far_far)).astype(BF16)
    there = lax.dynamic_index_in_dim(lax.all_gather(other, "pair", axis=0), 1 - core, 0, keepdims=False)
    mine_b = add(mine, there).astype(BF16)
    right_a = after(right_a, mine_b)
    mine_b = after(mine_b, right_a)
    moved_b = swap(mine_b, "sub", 2, 1)

    hidden = gelu(gain_in, mine_a, jnp.concatenate([left_a, right_a], axis=1))
    there = swap(hidden, "pair", 2, 1)
    first_core = core == 0
    hidden = jnp.concatenate([jnp.where(first_core, hidden, there), jnp.where(first_core, there, hidden)], axis=1)
    mlp_a = down_projection(hidden, w_down)
    terms_a = sent(mlp_a, n)
    kept = [lax.dynamic_slice_in_dim(part, z * rows, rows, 0) for part in (near_a, far_a)]
    kept = jnp.concatenate([jnp.where(odd, kept[1], kept[0]), jnp.where(odd, kept[0], kept[1])], axis=1)
    total = lax.dynamic_slice_in_dim(mlp_a, z * rows, rows, 0).astype(F32)
    for term in terms_a:
        total = total + term.astype(F32)
    done = (kept.astype(F32) + gain_down * total).astype(BF16)

    hidden = gelu(gain_in, mine_b, after(moved_b, mlp_a))
    hidden = lax.all_gather(hidden, "pair", axis=0)
    mlp_b = dot(jnp.concatenate([hidden[0], hidden[1]], axis=1), w_down).astype(BF16)
    return end(gain_down, done, near_b, far_b, mlp_b, sent(mlp_b, n))


def solution(mesh):
    shape = dict(mesh.shape)
    fast = shape["blk"] == 4 and shape["sub"] == 2 and shape["pair"] == 2
    in_specs = (
        P(("groups", "blk"), ("sub", "pair")),
        P("groups", "blk"),
        P("blk", ("sub", "pair")),
        P(("sub", "pair"), "blk"),
        P("blk", ("sub", "pair")),
        P(),
    )
    out_specs = P(("groups", "blk"), ("sub", "pair"))
    local = swapped if fast else general
    return jax.shard_map(local, mesh=mesh, in_specs=in_specs, out_specs=out_specs, check_vma=False)
```

```python
import functools
import math

import jax
import jax.numpy as jnp
from jax import lax
from jax.experimental import pallas as pl
from jax.experimental.pallas import tpu as pltpu
from jax.sharding import PartitionSpec as P

F32 = jnp.float32
BF16 = jnp.bfloat16


def general(resid, context, w_out, w_in, w_down, scales):
    attn = lax.psum_scatter(
        jnp.dot(context, w_out, preferred_element_type=F32).astype(BF16), "blk", scatter_dimension=0, tiled=True
    ).astype(F32)
    mixed = (resid.astype(F32) + scales[0] * attn).astype(BF16)
    pre_terms = jnp.dot(lax.all_gather(mixed, "blk", axis=0, tiled=True), w_in, preferred_element_type=F32)
    pre_part = lax.psum_scatter(
        pre_terms.astype(BF16), ("sub", "pair"), scatter_dimension=0, tiled=True
    ).astype(F32)
    hidden_part = jax.nn.gelu(scales[1] * pre_part, approximate=False).astype(BF16)
    hidden = lax.all_gather(hidden_part, ("sub", "pair"), axis=0, tiled=True)
    mlp = lax.psum_scatter(
        jnp.dot(hidden, w_down, preferred_element_type=F32).astype(BF16), "blk", scatter_dimension=0, tiled=True
    ).astype(F32)
    return (mixed.astype(F32) + scales[2] * mlp).astype(BF16)


def swap(x, axis, size, flip):
    return lax.ppermute(x, axis, [(i, i ^ flip) for i in range(size)])


def add(a, b):
    return a.astype(F32) + b.astype(F32)


def dot(x, w):
    return jnp.dot(x, w, preferred_element_type=F32)


def in_hbm(x):
    return pltpu.with_memory_space_constraint(x, pltpu.HBM)


ANY = pl.BlockSpec(memory_space=pl.ANY)
SMEM = pl.BlockSpec(memory_space=pltpu.SMEM)
VMEM = pl.BlockSpec(memory_space=pltpu.VMEM)


def nothing(*refs):
    pass


def after(x, *done):
    return pl.pallas_call(
        nothing,
        out_shape=jax.ShapeDtypeStruct(x.shape, x.dtype),
        in_specs=[ANY] * (1 + len(done)),
        out_specs=ANY,
        input_output_aliases={0: 0},
        compiler_params=pltpu.CompilerParams(vmem_limit_bytes=1 << 20),
    )(x, *done)


def sent(mlp, n):
    z = lax.axis_index("blk")
    blocks = mlp.reshape(n, mlp.shape[0] // n, -1)
    return [swap(lax.dynamic_index_in_dim(blocks, z ^ flip, 0, keepdims=False), "blk", n, flip) for flip in (3, 2, 1)]


def sent_by_two(mlp, n):
    z = lax.axis_index("blk")
    blocks = mlp.reshape(n, mlp.shape[0] // n, -1)

    def of(flip):
        return lax.dynamic_index_in_dim(blocks, z ^ flip, 0, keepdims=False)

    joint = swap(of(3), "blk", n, 1)
    term = swap(of(1), "blk", n, 1)
    return [term, swap(add(of(2), joint).astype(BF16), "blk", n, 2)]


def out_kernel(pieces, near, scales_hbm, ctx_hbm, w_hbm, res_hbm, *rest):
    parts, gains, (ctx, w, res, acc, scales, sems) = rest[:-8], rest[-8:-6], rest[-6:]
    depth, width = w.shape
    block = depth // pieces
    tile = min(256, width)
    z = lax.axis_index("blk")
    which = (z & 1) if near else 1 - (z & 1)
    columns = pl.ds(pl.multiple_of(which * width, width), width)
    loads = []
    for k in range(pieces):
        at = pl.ds(k * block, block)
        loads.append(
            (
                pltpu.make_async_copy(ctx_hbm.at[:, at], ctx.at[:, at], sems.at[2 + 2 * k]),
                pltpu.make_async_copy(w_hbm.at[at, columns], w.at[at], sems.at[3 + 2 * k]),
            )
        )
    last = (
        pltpu.make_async_copy(res_hbm.at[:, columns], res, sems.at[0]),
        pltpu.make_async_copy(scales_hbm, scales, sems.at[1]),
    )
    for load in [load for pair in loads for load in pair] + list(last):
        load.start()
    for k in range(pieces):
        for load in loads[k] + (last if k == pieces - 1 else ()):
            load.wait()
        deep = slice(k * block, (k + 1) * block)
        for c in range(width // tile):
            at = slice(c * tile, (c + 1) * tile)
            term = dot(ctx[:, deep], w[deep, at])
            if k:
                term = acc[:, at] + term
            if k < pieces - 1:
                acc[:, at] = term
                continue
            term = (term * scales[0]).reshape(-1, res.shape[0], tile)
            mine = lax.broadcasted_iota(jnp.int32, term.shape, 0) == z
            term = (term + jnp.where(mine, res[:, at].astype(F32)[None], 0.0)).astype(BF16)
            start = 0
            for part in parts:
                part[:, :, at] = term[:, start:start + part.shape[1]]
                start += part.shape[1]
    for index, gain in enumerate(gains):
        gain[...] = jnp.full_like(gain, scales[1 + index])


def out_projection(context, w_out, resid, scales, near, sizes):
    depth, width = w_out.shape[0], w_out.shape[1] // 2
    pieces = depth // 256
    n = context.shape[0] // resid.shape[0]
    gains = [jax.ShapeDtypeStruct((1, 128), F32), jax.ShapeDtypeStruct((1, 2 * width), F32)]
    *parts, gain_in, gain_down = pl.pallas_call(
        functools.partial(out_kernel, pieces, near),
        out_shape=[jax.ShapeDtypeStruct((n, size, width), BF16) for size in sizes] + gains,
        in_specs=[ANY] * 4,
        out_specs=[VMEM] * (len(sizes) + 2),
        scratch_shapes=[
            pltpu.VMEM(context.shape, BF16),
            pltpu.VMEM((depth, width), BF16),
            pltpu.VMEM((resid.shape[0], width), BF16),
            pltpu.VMEM((context.shape[0], width), F32),
            pltpu.SMEM(scales.shape, F32),
            pltpu.SemaphoreType.DMA((2 + 2 * pieces,)),
        ],
        compiler_params=pltpu.CompilerParams(vmem_limit_bytes=9 << 20),
        cost_estimate=pl.CostEstimate(
            flops=2 * context.shape[0] * depth * width, bytes_accessed=2 * depth * width, transcendentals=0
        ),
    )(in_hbm(scales), in_hbm(context), in_hbm(w_out), in_hbm(resid))
    return [part.reshape(n * size, width) for part, size in zip(parts, sizes)] + [gain_in, gain_down]


def fetch_kernel(w_hbm, done, *rest):
    parts, token, sems = rest[:-2], rest[-2], rest[-1]
    token[...] = jnp.zeros_like(token)
    height, width = parts[0].shape
    odd, core = lax.axis_index("blk") & 1, lax.axis_index("pair")
    blocks = [(odd, 1 - core), (odd, core), (1 - odd, 1 - core), (1 - odd, core)]
    loads = []
    for index, ((row, column), part) in enumerate(zip(blocks, parts)):
        at_row = pl.ds(pl.multiple_of(row * height, height), height)
        at_column = pl.ds(pl.multiple_of(column * width, width), width)
        loads.append(pltpu.make_async_copy(w_hbm.at[at_row, at_column], part, sems.at[index]))
        loads[index].start()
    for load in loads:
        load.wait()


def fetch(w, done):
    part = pltpu.VMEM((w.shape[0] // 2, w.shape[1] // 2), BF16)
    return pl.pallas_call(
        fetch_kernel,
        out_shape=[part] * 4 + [jax.ShapeDtypeStruct((8, 128), F32)],
        in_specs=[ANY, ANY],
        out_specs=[VMEM] * 5,
        scratch_shapes=[pltpu.SemaphoreType.DMA((4,))],
        compiler_params=pltpu.CompilerParams(vmem_limit_bytes=2 << 20),
        cost_estimate=pl.CostEstimate(flops=0, bytes_accessed=1024, transcendentals=0),
    )(in_hbm(w), done)


def gelu_kernel(gain, own, there, out):
    tile = 256
    for start in range(0, out.shape[1], tile):
        at = slice(start, min(start + tile, out.shape[1]))
        v = gain[:1, :1] * add(own[:, at], there[:, at])
        out[:, at] = (0.5 * v * (1.0 + lax.erf(v * math.sqrt(0.5)))).astype(BF16)


def gelu(gain, own, there):
    return pl.pallas_call(
        gelu_kernel,
        out_shape=jax.ShapeDtypeStruct(own.shape, BF16),
        in_specs=[VMEM] * 3,
        out_specs=VMEM,
        compiler_params=pltpu.CompilerParams(vmem_limit_bytes=3 << 20),
    )(gain, own, there)


def down_kernel(pieces, hidden, w_hbm, out, w, acc, sems):
    depth, width = w.shape
    block, tile = depth // pieces, min(512, width)
    loads = []
    for k in range(pieces):
        at = pl.ds(k * block, block)
        loads.append(pltpu.make_async_copy(w_hbm.at[at], w.at[at], sems.at[k]))
        loads[k].start()
    for k in range(pieces):
        loads[k].wait()
        deep = slice(k * block, (k + 1) * block)
        for c in range(width // tile):
            at = slice(c * tile, (c + 1) * tile)
            term = dot(hidden[:, deep], w[deep, at])
            if k:
                term = acc[:, at] + term
            if k < pieces - 1:
                acc[:, at] = term
            else:
                out[:, at] = term.astype(BF16)


def down_projection(hidden, w):
    rows, width = hidden.shape[0], w.shape[1]
    pieces = w.shape[0] // 256
    return pl.pallas_call(
        functools.partial(down_kernel, pieces),
        out_shape=jax.ShapeDtypeStruct((rows, width), BF16),
        in_specs=[VMEM, ANY],
        out_specs=VMEM,
        scratch_shapes=[
            pltpu.VMEM(w.shape, BF16),
            pltpu.VMEM((rows, width), F32),
            pltpu.SemaphoreType.DMA((pieces,)),
        ],
        compiler_params=pltpu.CompilerParams(vmem_limit_bytes=18 << 20),
        cost_estimate=pl.CostEstimate(flops=2 * rows * w.size, bytes_accessed=2 * w.size, transcendentals=0),
    )(hidden, in_hbm(w))


def end_kernel(gain, done, near, far, mlp, first, second, third, out):
    z = lax.axis_index("blk")
    odd = (z & 1) == 1
    size, width = first.shape[0], out.shape[1] // 2
    rows = pl.ds(pl.multiple_of(z * size, size), size)
    head = out.shape[0] - size
    out[:head, :] = done[...]
    for part in range(2):
        at = slice(part * width, (part + 1) * width)
        total = mlp[rows, at].astype(F32)
        for term in (first, second, third):
            total = total + term[:, at].astype(F32)
        other, own = (far, near) if part == 0 else (near, far)
        mixed = jnp.where(odd, other[rows, :].astype(F32), own[rows, :].astype(F32))
        out[head:, at] = (mixed + gain[:1, :1] * total).astype(BF16)


def end(gain, done, near, far, mlp, terms):
    rows, width = done.shape[0] + terms[0].shape[0], done.shape[1]
    return pl.pallas_call(
        end_kernel,
        out_shape=jax.ShapeDtypeStruct((rows, width), BF16),
        in_specs=[VMEM] * 8,
        out_specs=VMEM,
        compiler_params=pltpu.CompilerParams(vmem_limit_bytes=3 << 20),
    )(gain, done, near, far, mlp, *terms)


def swapped(resid, context, w_out, w_in, w_down, scales):
    n = 4
    z, core = lax.axis_index("blk"), lax.axis_index("pair")
    odd = (z & 1) == 1
    rows = resid.shape[0] // 2
    sizes = [rows, rows]

    other_a, other_b, _, _ = out_projection(context, w_out, resid, scales, False, sizes)
    own_a, own_b, gain_in, gain_down = out_projection(context, w_out, resid, scales, True, sizes)
    other_b = after(other_b, own_a)
    sum_a = add(own_a, swap(other_a, "blk", n, 1)).astype(BF16)
    sum_b = add(own_b, swap(other_b, "blk", n, 1)).astype(BF16)
    near_far, near_near, far_far, far_near, fetched = fetch(w_in, sum_a)

    crossed = after(swap(sum_a, "blk", n, 2), fetched, sum_b)
    near_a = add(sum_a, crossed).astype(BF16)
    first = dot(near_a, near_far)
    sum_b = after(sum_b, first)
    far_a = swap(near_a, "blk", n, 1)
    crossed = swap(sum_b, "blk", n, 2)
    other = (first + dot(far_a, far_far)).astype(BF16)
    mine = dot(near_a, near_near)
    mine = mine + dot(far_a, far_near)
    early = mine
    mine_a = add(mine, swap(other, "pair", 2, 1)).astype(BF16)

    crossed = after(crossed, other, early)
    near_b = add(sum_b, crossed).astype(BF16)
    width = mine_a.shape[1] // 128 * 3 // 8 * 128
    left_a = swap(mine_a[:, :width], "sub", 2, 1)
    right_a = swap(mine_a[:, width:], "sub", 2, 1)
    far_b = after(swap(near_b, "blk", n, 1), left_a)
    mine = dot(near_b, near_near)
    first = dot(near_b, near_far)
    far_b = after(far_b, mine, first)
    mine = mine + dot(far_b, far_near)
    other = (first + dot(far_b, far_far)).astype(BF16)
    there = lax.dynamic_index_in_dim(lax.all_gather(other, "pair", axis=0), 1 - core, 0, keepdims=False)
    mine_b = add(mine, there).astype(BF16)
    right_a = after(right_a, mine_b)
    mine_b = after(mine_b, right_a)
    moved_b = swap(mine_b, "sub", 2, 1)

    hidden = gelu(gain_in, mine_a, jnp.concatenate([left_a, right_a], axis=1))
    there = swap(hidden, "pair", 2, 1)
    first_core = core == 0
    hidden = jnp.concatenate([jnp.where(first_core, hidden, there), jnp.where(first_core, there, hidden)], axis=1)
    mlp_a = down_projection(hidden, w_down)
    terms_a = sent(mlp_a, n)
    kept = [lax.dynamic_slice_in_dim(part, z * rows, rows, 0) for part in (near_a, far_a)]
    kept = jnp.concatenate([jnp.where(odd, kept[1], kept[0]), jnp.where(odd, kept[0], kept[1])], axis=1)
    total = lax.dynamic_slice_in_dim(mlp_a, z * rows, rows, 0).astype(F32)
    for term in terms_a:
        total = total + term.astype(F32)
    done = (kept.astype(F32) + gain_down * total).astype(BF16)

    hidden = gelu(gain_in, mine_b, after(moved_b, mlp_a))
    hidden = lax.all_gather(hidden, "pair", axis=0)
    mlp_b = dot(jnp.concatenate([hidden[0], hidden[1]], axis=1), w_down).astype(BF16)
    return end(gain_down, done, near_b, far_b, mlp_b, sent(mlp_b, n))


def solution(mesh):
    shape = dict(mesh.shape)
    fast = shape["blk"] == 4 and shape["sub"] == 2 and shape["pair"] == 2
    in_specs = (
        P(("groups", "blk"), ("sub", "pair")),
        P("groups", "blk"),
        P("blk", ("sub", "pair")),
        P(("sub", "pair"), "blk"),
        P("blk", ("sub", "pair")),
        P(),
    )
    out_specs = P(("groups", "blk"), ("sub", "pair"))
    local = swapped if fast else general
    return jax.shard_map(local, mesh=mesh, in_specs=in_specs, out_specs=out_specs, check_vma=False)
```
